512 devices in a mesh: ctx: 64 (over x, z, core), tp: 8 (over y).
Axes of the slice: x: 4, y: 8, z: 8, core: 2. Of those that a mesh axis runs over, the one named last changes fastest.
Arguments:
- kv_cache: bfloat16 [262144, 2048], P('ctx', 'tp'), may hold values from -6 to 6
- page_session: int32 [4096], P('ctx'), may hold values from 0 to 3
- queries: bfloat16 [256, 8192], P(None, 'tp'), may hold values from -12 to 12
- tree_kv: bfloat16 [256, 2048], P(None, 'tp'), may hold values from -12 to 12
- tree_parent: int32 [4, 64], replicated, may hold values from -1 to 62, as said below
- move_count: int32 [64, 64], replicated, may hold values from 0 to 1, as said below
- draft_states: bfloat16 [256, 4096], P(None, 'ctx'), may hold values from -20 to 20
- accept_node: int32 [4, 8], replicated, may hold values from 0 to 63
- w_gate: bfloat16 [4096, 14336], P('ctx', 'tp'), may hold values from -0.09375 to 0.09375
- w_up: bfloat16 [4096, 14336], P('ctx', 'tp'), may hold values from -0.09375 to 0.09375
- w_down: bfloat16 [14336, 4096], P('tp', 'ctx'), may hold values from -0.046875 to 0.046875
Outputs:
- attn_out: bfloat16 [256, 8192], P('ctx', 'tp')
- arrived: bfloat16 [131072, 2048], P('ctx', 'tp')
- draft_out: bfloat16 [32, 4096], P(None, 'ctx')
The draws below stay inside these ranges and needn't reach their ends.
Inputs may be any that keep to these rules, and one draw needn't show every extreme that they name: Each tree_parent[s, i] is -1 or a node below i. `move_count`: each shard sends to at most 32 shards and receives from at most 32; every row and every column sums to at most 32, and some row and some column reach it.
All inputs are finite; a program needn't handle non-finite values.
Results may differ from the reference program's by a relative error of at most 0.005.
Values may be sent and summed in bfloat16 or wider, within the bound.
A program may use at most 128 MiB of HBM per device.

```python
import math
import jax
import jax.numpy as jnp
from jax import lax

HD = 128
QH = 64
KVH = 8
DD = 4096
DFF = 14336
PAGE = 64
PAGES_DEV = 64
SESS = 4
BR = 8
MOVE_PAIR = 1
SHARDS = 64
MOVE_SPAN = 32
NODES = 64
ROWS = 256
RECV_CAP = 32
CTX_TOK = 262144


def draw_kv_cache(key, part):
    own_key = jax.random.fold_in(key, 3)
    shape = (CTX_TOK, KVH * 2 * HD)
    base = jnp.clip(jax.random.normal(own_key, shape, jnp.float32), -6.0, 6.0)
    return base.astype(jnp.bfloat16)


def draw_queries(key, part):
    own_key = jax.random.fold_in(key, 5)
    shape = (ROWS, QH * HD)
    base = jnp.clip(3.0 * jax.random.normal(own_key, shape, jnp.float32), -12.0, 12.0)
    return base.astype(jnp.bfloat16)


def draw_tree_kv(key, part):
    own_key = jax.random.fold_in(key, 7)
    shape = (ROWS, KVH * 2 * HD)
    column = jnp.arange(shape[1])[None, :]
    spread = jnp.where(column // HD % 2 == 0, 3.0, 1.0)
    base = jnp.clip(jax.random.normal(own_key, shape, jnp.float32), -4.0, 4.0)
    return (base * spread).astype(jnp.bfloat16)


def draw_draft_states(key, part):
    own_key = jax.random.fold_in(key, 11)
    shape = (ROWS, DD)
    column = jnp.arange(DD)[None, :].astype(jnp.float32)
    spread = jnp.exp(jnp.log(3.0) * column / DD)
    base = jnp.clip(jax.random.normal(own_key, shape, jnp.float32), -6.0, 6.0)
    return jnp.clip(base * spread, -20.0, 20.0).astype(jnp.bfloat16)


def draw_tree_parent(key, part):
    own_key = jax.random.fold_in(key, 13)
    raw = jax.random.randint(own_key, (SESS, NODES), 0, 1 << 20)
    node = jnp.arange(NODES, dtype=jnp.int32)[None, :]
    parent = raw % (node + 1) - 1
    parent = parent.at[0, NODES - 1].set(NODES - 2)
    return parent.astype(jnp.int32)


def draw_move_count(key, part):
    own_key = jax.random.fold_in(key, 17)
    keys = jax.random.split(own_key, 5)
    sigma = jax.random.permutation(keys[0], SHARDS)
    tau = jax.random.permutation(keys[1], SHARDS)
    amount = (jax.random.randint(keys[2], (SHARDS, MOVE_SPAN), 0, 4) > 0).astype(jnp.int32)
    heavy_source = jax.random.randint(keys[3], (), 0, SHARDS)
    heavy_dest = jax.random.randint(keys[4], (), 0, SHARDS)
    source = jnp.arange(SHARDS, dtype=jnp.int32)[:, None]
    offset = jnp.arange(MOVE_SPAN, dtype=jnp.int32)[None, :]
    dest = sigma[(tau[source] + offset) % SHARDS]
    amount = jnp.where(source == heavy_source, MOVE_PAIR, amount)
    amount = jnp.where(dest == heavy_dest, MOVE_PAIR, amount)
    sources = jnp.broadcast_to(source, dest.shape)
    counts = jnp.zeros((SHARDS, SHARDS), jnp.int32).at[sources, dest].add(amount)
    return counts.astype(jnp.int32)


def plant(values, stream_key, smallest, largest):
    longest = values.shape.index(max(values.shape))
    spots = []
    for shift in (0, 1):
        where = [jax.random.randint(jax.random.fold_in(stream_key, axis), (), 0, length) for axis, length in enumerate(values.shape)]
        where[longest] = (where[longest] + shift) % values.shape[longest]
        spots.append(tuple(where))
    return values.at[spots[0]].set(smallest).at[spots[1]].set(largest)


def level_of(key, shape, cuts, least, largest):
    def one(dim, parts):
        steps = jax.random.uniform(jax.random.fold_in(jax.random.fold_in(key, 6), dim), (parts,), jnp.float32, least / len(cuts), largest / len(cuts))
        return jnp.repeat(jnp.exp(steps), shape[dim] // parts).reshape((-1,) + (1,) * (len(shape) - dim - 1))

    gain = one(*cuts[0])
    for cut in cuts[1:]:
        gain = gain * one(*cut)
    return gain


def scatter_about(key, dims, scale, bound, pieces=(), kind=jnp.bfloat16):
    gain = level_of(key, dims, pieces, -0.22, 0.18) if pieces else 1.0
    values = jax.random.normal(key, dims, jnp.float32) * scale * gain
    return jnp.minimum(jnp.maximum(values, -bound), bound).astype(kind)


def setup_inputs(seed: int = 0) -> dict:
    streams_of = jax.random.split(jax.random.key(seed), 12)
    return {
        "kv_cache": draw_kv_cache(jax.random.fold_in(streams_of[11], 71), 0),
        "page_session": plant(jax.random.randint(streams_of[1], (SHARDS * PAGES_DEV,), 0, SESS), jax.random.fold_in(streams_of[1], 1), 0, SESS - 1).astype(jnp.int32),
        "queries": draw_queries(jax.random.fold_in(streams_of[11], 71), 0),
        "tree_kv": draw_tree_kv(jax.random.fold_in(streams_of[11], 71), 0),
        "tree_parent": draw_tree_parent(jax.random.fold_in(streams_of[11], 71), 0),
        "move_count": draw_move_count(jax.random.fold_in(streams_of[11], 71), 0),
        "draft_states": draw_draft_states(jax.random.fold_in(streams_of[11], 71), 0),
        "accept_node": plant(jax.random.randint(streams_of[7], (SESS, BR), 0, NODES), jax.random.fold_in(streams_of[7], 1), 0, NODES - 1).astype(jnp.int32),
        "w_gate": scatter_about(streams_of[8], (DD, DFF), DD ** -0.5, 0.09375, ((0, 64), (1, 8))),
        "w_up": scatter_about(streams_of[9], (DD, DFF), DD ** -0.5, 0.09375, ((0, 64), (1, 8))),
        "w_down": scatter_about(streams_of[10], (DFF, DD), DFF ** -0.5, 0.046875, ((0, 8), (1, 64))),
    }


def ancestors(parents):
    count = parents.shape[0]
    nodes = jnp.arange(count, dtype=jnp.int32)
    link = (parents[:, None] == nodes[None, :]).astype(jnp.float32)
    reach = link + jnp.eye(count, dtype=jnp.float32)
    for repeat in range(count.bit_length()):
        reach = jnp.minimum(jnp.dot(reach, reach, precision=lax.Precision.HIGHEST), 1.0)
    return reach

def reference(kv_cache, page_session, queries, tree_kv, tree_parent, move_count, draft_states, accept_node, w_gate, w_up, w_down):
    group = QH // KVH
    scale = 1.0 / math.sqrt(HD)
    token_session = jnp.repeat(page_session, PAGE)
    reach = jax.vmap(ancestors)(tree_parent) > 0.5

    def one_head(head_index):
        base = head_index * 2 * HD
        keys = lax.dynamic_slice_in_dim(kv_cache, base, HD, 1)
        values = lax.dynamic_slice_in_dim(kv_cache, base + HD, HD, 1)
        tree_keys = lax.dynamic_slice_in_dim(tree_kv, base, HD, 1)
        tree_values = lax.dynamic_slice_in_dim(tree_kv, base + HD, HD, 1)
        heads = lax.dynamic_slice_in_dim(queries, head_index * group * HD, group * HD, 1)

        def one_session(session):
            rows = lax.dynamic_slice_in_dim(heads, session * NODES, NODES, 0).reshape(NODES * group, HD)
            own_keys = lax.dynamic_slice_in_dim(tree_keys, session * NODES, NODES, 0)
            own_values = lax.dynamic_slice_in_dim(tree_values, session * NODES, NODES, 0)
            scores = jnp.einsum('qd,kd->qk', rows, keys, preferred_element_type=jnp.float32) * scale
            scores = jnp.where(token_session[None, :] == session, scores, -jnp.inf)
            branch = jnp.einsum('qd,kd->qk', rows, own_keys, preferred_element_type=jnp.float32) * scale
            allowed = jnp.repeat(reach[session], group, axis=0)
            branch = jnp.where(allowed, branch, -jnp.inf)
            top = jnp.maximum(lax.optimization_barrier(jnp.max(scores, axis=1)), lax.optimization_barrier(jnp.max(branch, axis=1)))
            weights = jnp.exp(scores - top[:, None])
            tree_weights = jnp.exp(branch - top[:, None])
            total = lax.optimization_barrier(jnp.sum(weights, axis=1)) + lax.optimization_barrier(jnp.sum(tree_weights, axis=1))
            mixed = jnp.dot(weights.astype(jnp.bfloat16), values, preferred_element_type=jnp.float32)
            mixed = mixed + jnp.dot(tree_weights.astype(jnp.bfloat16), own_values, preferred_element_type=jnp.float32)
            return (mixed / total[:, None]).reshape(NODES, group * HD)
        return lax.map(one_session, jnp.arange(SESS, dtype=jnp.int32)).reshape(ROWS, group * HD)
    per_head = lax.map(one_head, jnp.arange(KVH, dtype=jnp.int32))
    attn_out = jnp.transpose(per_head, (1, 0, 2)).reshape(ROWS, QH * HD).astype(jnp.bfloat16)
    width = kv_cache.shape[1]
    pages = kv_cache.reshape(SHARDS, PAGES_DEV, PAGE, width)
    send_start = jnp.cumsum(move_count, axis=1) - move_count
    recv_end = jnp.cumsum(move_count, axis=0)
    recv_start = recv_end - move_count
    slots = jnp.arange(RECV_CAP, dtype=jnp.int32)

    def one_dest(dest):
        ends = recv_end[:, dest]
        source = lax.optimization_barrier(jnp.sum((ends[None, :] <= slots[:, None]).astype(jnp.int32), axis=1))
        valid = slots < ends[SHARDS - 1]
        source = jnp.minimum(source, SHARDS - 1)
        offset = slots - recv_start[source, dest]
        local = jnp.clip(send_start[source, dest] + offset, 0, PAGES_DEV - 1)
        picked = pages[source, local]
        return jnp.where(valid[:, None, None], picked, jnp.zeros_like(picked))
    arrived = lax.map(one_dest, jnp.arange(SHARDS, dtype=jnp.int32)).reshape(SHARDS * RECV_CAP * PAGE, width)
    rows_index = (jnp.arange(SESS, dtype=jnp.int32)[:, None] * NODES + accept_node).reshape(-1)
    chosen = draft_states[rows_index]
    widened = chosen.astype(jnp.float32)
    inverse = lax.rsqrt(lax.optimization_barrier(jnp.mean(widened * widened, axis=1)) + 1e-05)
    gate = inverse[:, None] * jnp.dot(chosen, w_gate, preferred_element_type=jnp.float32)
    up_proj = inverse[:, None] * jnp.dot(chosen, w_up, preferred_element_type=jnp.float32)
    hidden = (jax.nn.silu(gate) * up_proj).astype(jnp.bfloat16)
    draft_out = jnp.dot(hidden, w_down, preferred_element_type=jnp.float32).astype(jnp.bfloat16)
    return (attn_out, arrived, draft_out)
```

```python
import math

import jax
import jax.numpy as jnp
from jax import lax
from jax.experimental import pallas as pl
from jax.experimental.pallas import tpu as pltpu
from jax.sharding import PartitionSpec as P

MESH = pl.DeviceIdType.MESH
F32 = jnp.float32
BF16 = jnp.bfloat16

HD = 128
HEADS = 8
PAGE = 64
NODES = 64
SESS = 4
DD = 4096
XS, ZS, CS, TP = 4, 8, 2, 8
CHUNK = 512
FAR = -1e30
UNIT = math.log2(math.e) / math.sqrt(HD)
HALF = 896

F_CORE, F_X, F_Z = 0, 0, 3
G_CORE, G_Z, G_X, G_TP = 11, 11, 18, 21
A_CORE, A_XO, A_XW, A_ZO, A_ZW, A_FIN = 29, 32, 35, 38, 45, 53
M_CORE, M_X, M_Z = 54, 55, 61
COPIES = 61 + 8 * 7


def dot_nt(a, b):
    return lax.dot_general(a, b, (((1,), (1,)), ((), ())), preferred_element_type=F32)


def dot_nn(a, b):
    return jnp.dot(a, b, preferred_element_type=F32)


def merge(parts):
    n = parts[0][1].shape[0]
    spot = lax.broadcasted_iota(jnp.int32, (n, 128), 1)
    top = parts[0][1]
    for part in parts[1:]:
        top = jnp.maximum(top, part[1])
    total = None
    sums = [None] * 4
    for value, info in parts:
        factor = jnp.exp2(info - top)
        term = info * pltpu.roll(factor, 4, 1)
        total = term if total is None else total + term
        for i in range(4):
            term = value[i] * factor[:, i : i + 1]
            sums[i] = term if sums[i] is None else sums[i] + term
    return sums, jnp.where(spot < 4, top, jnp.where(spot < 8, total, 0.0))


def narrow(info):
    packed = info[0:8]
    for k in range(1, ZS):
        packed = packed + pltpu.roll(info[k * 8 : k * 8 + 8], 16 * k, 1)
    return packed


def widen(packed):
    spot = lax.broadcasted_iota(jnp.int32, (8, 128), 1)
    rows = [packed] + [pltpu.roll(packed, 128 - 16 * k, 1) for k in range(1, ZS)]
    return jnp.concatenate([jnp.where(spot < 8, row, 0.0) for row in rows], axis=0)


def kernel(
    kv, ps, q, tkv, parent, mc, states, accept, wg, wu, wd,
    attn_out, zin, draft_out,
    q2, bias, scores, mx, acc, tot,
    give0, give1, give2, give3, mine, core_in0, core_in1, core_in2, core_in3,
    xo0, xo1, xo2, xw0, xw1, xw2, xo_in, xw_in, zo, zw, zo_in, zw_in, fin, fin_in,
    f_out, f_core, f_b, f_x, f_s, f_z, h_own, h_z, h_s, h_x, h_t, h_c, hbf, d_own, d_in,
    to_core, own_pages, from_core, xin0, xin1, xin2, xin3, xin4, xin5,
    ssem, rsem, lsem,
):
    give = [give0, give1, give2, give3]
    core_in = [core_in0, core_in1, core_in2, core_in3]
    xo, xw = [xo0, xo1, xo2], [xw0, xw1, xw2]
    xin = [xin0, xin1, xin2, xin3, xin4, xin5]
    me = lax.axis_index("ctx")
    y = lax.axis_index("tp")
    x = me // 16
    z = lax.rem(me // 2, 8)
    c = lax.rem(me, 2)

    def ctx_at(px, pz, pc):
        return {"ctx": px * 16 + pz * 2 + pc}

    core_peer = ctx_at(x, z, 1 - c)

    def x_at(k):
        return lax.rem(x + k, XS)

    def z_at(k):
        return lax.rem(z + k, ZS)

    def x_peer(k):
        return ctx_at(x_at(k), z, c)

    def z_peer(k):
        return ctx_at(x, z_at(k), c)

    def y_peer(k):
        return {"tp": lax.rem(y + k, TP)}

    sent = []

    def send(src, dst, i, peer):
        cp = pltpu.make_async_remote_copy(
            src_ref=src, dst_ref=dst, send_sem=ssem.at[i], recv_sem=rsem.at[i],
            device_id=peer, device_id_type=MESH,
        )
        cp.start()
        sent.append(cp)
        return cp

    def arrive(cps):
        for cp in cps:
            cp.wait_recv()

    barrier = pltpu.get_barrier_semaphore()
    peers = [core_peer] + [z_peer(k) for k in range(1, ZS)]
    peers += [x_peer(k) for k in range(1, XS)] + [y_peer(k) for k in range(1, TP)]
    for peer in peers:
        pl.semaphore_signal(barrier, inc=1, device_id=peer, device_id_type=MESH)

    def pack(k, start):
        first = start
        second = start + mc[me, 2 * k]
        own = jnp.where(c == 0, first, second)
        other = jnp.where(c == 0, second, first)
        px, pz = k // ZS, lax.rem(k, ZS)
        own_pages[px, pz] = kv[own]
        to_core[px, pz] = kv[other]
        return second + mc[me, 2 * k + 1]

    lax.fori_loop(0, 32, pack, jnp.int32(0))

    sub = lax.broadcasted_iota(jnp.int32, (32, 256), 0)
    lane = lax.broadcasted_iota(jnp.int32, (32, 256), 1)
    row_of = jnp.zeros((32, 256), jnp.int32)
    for r in range(32):
        row_of = jnp.where(sub == r, accept[r // 8, r % 8] + (r // 8) * NODES, row_of)
    pick = jnp.where(lane == row_of, 1.0, 0.0).astype(BF16)
    chosen = dot_nt(pick, states[...])
    squares = jnp.broadcast_to(jnp.sum(chosen * chosen, axis=1, keepdims=True), (32, 256))
    chosen = chosen.astype(BF16)
    for half in range(2):
        gate = dot_nn(chosen, wg[:, half * HALF : (half + 1) * HALF])
        up = dot_nn(chosen, wu[:, half * HALF : (half + 1) * HALF])
        for px in range(XS):
            rows = slice(px * 8, px * 8 + 8)
            for j in range(7):
                cols = slice(j * 128, j * 128 + 128)
                f_out[half, px, j, :, 0:128] = gate[rows, cols]
                f_out[half, px, j, :, 128:256] = up[rows, cols]
            f_out[half, px, 7] = squares[rows, :]

    pl.semaphore_wait(barrier, len(peers))

    z_order = (1, 7, 2, 6, 3, 5, 4)
    m_z = []
    kept = []

    def send_group(src, group, lead=()):
        for k in z_order:
            m_z.append(
                send(src.at[(*lead, z_at(k))], zin.at[k, group], M_Z + group * 7 + k - 1, z_peer(k))
            )
        cp = pltpu.make_async_copy(src.at[(*lead, z)], zin.at[0, group], lsem.at[group])
        cp.start()
        kept.append(cp)

    f_cp = send(f_out.at[1 - c], f_core, F_CORE + 3, core_peer)
    m_core = send(to_core, from_core, M_CORE, core_peer)
    send_group(own_pages, 0, (x,))

    for s in range(SESS):
        for h in range(HEADS):
            q2[s, h * NODES : (h + 1) * NODES, :] = q[
                s * NODES : (s + 1) * NODES, h * HD : (h + 1) * HD
            ]
    lane1 = lax.broadcasted_iota(jnp.int32, (1, 128), 1)
    for t in range(32):
        session = jnp.where(lane1 < PAGE, ps[2 * t], ps[2 * t + 1])
        for s in range(SESS):
            bias[s, :, t * 128 : (t + 1) * 128] = jnp.where(session == s, 0.0, FAR).astype(F32)

    m_x = {}

    def send_x(k, part):
        src = own_pages if part == 0 else from_core
        m_x[k, part] = send(
            src.at[x_at(k)], xin[(k - 1) * 2 + part], M_X + (k - 1) * 2 + part, x_peer(k)
        )

    def forward(k, part):
        m_x[k, part].wait_recv()
        send_group(xin[(k - 1) * 2 + part], k * 2 + part)

    def attend(n, k):
        s = x_at(k)
        rows = q2[s]
        mx[...] = jnp.full((512, 128), FAR, F32)

        def first(t, carry):
            at = pl.ds(pl.multiple_of(t * CHUNK, CHUNK), CHUNK)
            pages = pl.ds(t * (CHUNK // PAGE), CHUNK // PAGE)
            keys = kv[pages, :, 0:HD].reshape(CHUNK, HD)
            part = dot_nt(rows, keys) + bias[s, :, at]
            scores[:, at] = part
            top = mx[...]
            for i in range(CHUNK // 128):
                top = jnp.maximum(top, part[:, i * 128 : (i + 1) * 128])
            mx[...] = top
            return carry

        lax.fori_loop(0, 4096 // CHUNK, first, 0)
        top = jnp.max(mx[...], axis=1, keepdims=True) * UNIT
        mx[...] = jnp.broadcast_to(top, (512, 128))
        acc[...] = jnp.zeros((512, 128), F32)
        tot[...] = jnp.zeros((512, 128), F32)

        def second(t, carry):
            at = pl.ds(pl.multiple_of(t * CHUNK, CHUNK), CHUNK)
            pages = pl.ds(t * (CHUNK // PAGE), CHUNK // PAGE)
            weight = jnp.exp2(scores[:, at] * UNIT - top)
            part = weight[:, 0:128]
            for i in range(1, CHUNK // 128):
                part = part + weight[:, i * 128 : (i + 1) * 128]
            tot[...] = tot[...] + part
            values = kv[pages, :, HD : 2 * HD].reshape(CHUNK, HD)
            acc[...] = acc[...] + dot_nn(weight.astype(BF16), values)
            return carry

        lax.fori_loop(0, 4096 // CHUNK, second, 0)
        tot[...] = jnp.broadcast_to(jnp.sum(tot[...], axis=1, keepdims=True), (512, 128))
        spot = lax.broadcasted_iota(jnp.int32, (NODES, 128), 1)
        for part, group in ((give[n], 1 - c), (mine.at[n], c)):
            info = jnp.zeros((NODES, 128), F32)
            for i in range(4):
                at = pl.ds(pl.multiple_of(group * 256 + i * NODES, NODES), NODES)
                part[i] = acc[at, :]
                info = jnp.where(spot == i, mx[at, :], info)
                info = jnp.where(spot == 4 + i, tot[at, :], info)
            part[4] = info
        return send(give[n], core_in[n], A_CORE + n if n < 3 else A_FIN - 1, core_peer)

    def part_of(ref):
        return [ref[i] for i in range(4)], ref[4]

    a_x = []

    def join(n, k, cp):
        cp.wait_recv()
        sums, info = merge([part_of(mine.at[n]), part_of(core_in[n])])
        if k == 0:
            for i in range(4):
                mine[n, i] = sums[i]
            mine[n, 4] = info
            return
        for i in range(4):
            xo[n][i * NODES : (i + 1) * NODES, :] = sums[i].astype(BF16)
        xw[n][...] = narrow(info)
        a_x.append(send(xo[n], xo_in.at[k - 1], A_XO + k - 1, x_peer(k)))
        a_x.append(send(xw[n], xw_in.at[k - 1], A_XW + k - 1, x_peer(k)))

    a0 = attend(0, 1)

    f_cp.wait_recv()
    for px in range(XS):
        f_b[px] = (f_core[px] + f_out[c, px]).reshape(64, 256)
    f_xs = [send(f_b.at[x_at(k)], f_x.at[k - 1], F_X + k - 1, x_peer(k)) for k in range(1, XS)]
    send_x(1, 0)
    send_x(3, 0)
    m_core.wait_recv()
    send_group(from_core, 1, (x,))
    join(0, 1, a0)
    send_x(1, 1)
    send_x(3, 1)

    a1 = attend(1, 3)

    arrive(f_xs)
    whole = f_b[x]
    for k in range(XS - 1):
        whole = whole + f_x[k]
    for j in range(ZS):
        f_s[j, :, 0:256] = whole[j * 8 : j * 8 + 8]
        f_s[j, :, 256:384] = whole[56:64, 0:128]
    f_zs = [send(f_s.at[z_at(k)], f_z.at[k - 1], F_Z + k, z_peer(k)) for k in range(1, ZS)]
    join(1, 3, a1)
    send_x(2, 0)

    a2 = attend(2, 2)

    arrive(f_zs)
    whole = f_s[z]
    for k in range(ZS - 1):
        whole = whole + f_z[k]
    inverse = lax.rsqrt(whole[:, 256:384] / DD + 1e-05)
    gate = inverse * whole[:, 0:128]
    up = inverse * whole[:, 128:256]
    hidden = gate / (1.0 + jnp.exp(-gate)) * up
    h_own[...] = hidden.astype(BF16).astype(F32)
    g_zs = [send(h_own, h_z.at[k - 1], G_Z + k, z_peer(k)) for k in range(1, ZS)]
    join(2, 2, a2)
    send_x(2, 1)
    forward(1, 0)
    forward(3, 0)

    a3 = attend(3, 0)

    arrive(g_zs)
    for j in range(7):
        slot = lax.rem(z - j + ZS, ZS)
        h_s[j] = jnp.where(slot == 0, h_own[...], h_z[jnp.maximum(slot - 1, 0)])
    g_xs = [send(h_s, h_x.at[k - 1], G_X + k, x_peer(k)) for k in range(1, XS)]
    join(3, 0, a3)
    forward(1, 1)
    forward(3, 1)

    link_at = lax.broadcasted_iota(jnp.int32, (NODES, NODES), 0)
    node_at = lax.broadcasted_iota(jnp.int32, (NODES, NODES), 1)
    link = jnp.where((parent[pl.ds(x, 1), :] == link_at) | (link_at == node_at), 1.0, 0.0)
    for repeat in range(6):
        link = jnp.minimum(dot_nn(link.astype(BF16), link.astype(BF16)), 1.0)
    own_row = lax.broadcasted_iota(jnp.int32, (32, NODES), 0)
    own_node = lax.broadcasted_iota(jnp.int32, (32, NODES), 1)
    own = jnp.where(own_node == z * 8 + lax.rem(own_row, 8), 1.0, 0.0).astype(BF16)
    reach = dot_nt(own, link.astype(BF16)) > 0.5
    block = pl.ds(pl.multiple_of(x * NODES, NODES), NODES)
    picks = []
    for i in range(4):
        rows = q2[x, pl.ds(pl.multiple_of(c * 256 + i * NODES, NODES), NODES), :]
        picks.append(dot_nn(own[0:8], rows))
    q_own = jnp.concatenate(picks, axis=0).astype(BF16)
    branch = jnp.where(reach, dot_nt(q_own, tkv[block, 0:HD]) * UNIT, FAR)
    tree_top = jnp.max(branch, axis=1, keepdims=True)
    weight = jnp.exp2(branch - tree_top)
    tree_total = jnp.sum(weight, axis=1, keepdims=True)
    tree_sum = dot_nn(weight.astype(BF16), tkv[block, HD : 2 * HD])
    spot8 = lax.broadcasted_iota(jnp.int32, (8, 128), 1)
    info = jnp.zeros((8, 128), F32)
    for i in range(4):
        at = slice(i * 8, i * 8 + 8)
        info = jnp.where(spot8 == i, tree_top[at], info)
        info = jnp.where(spot8 == 4 + i, tree_total[at], info)
    tree_part = ([tree_sum[i * 8 : i * 8 + 8] for i in range(4)], info)

    arrive(g_xs)
    for px in range(XS):
        slot = lax.rem(x - px + XS, XS)
        h_t[px] = jnp.where(slot == 0, h_s[...], h_x[jnp.maximum(slot - 1, 0)])
    g_c = send(h_t, h_c, G_CORE, core_peer)

    arrive(a_x)
    parts = [part_of(mine.at[3])]
    for k in range(XS - 1):
        value = xo_in[k].astype(F32)
        parts.append(
            ([value[i * NODES : (i + 1) * NODES] for i in range(4)], widen(xw_in[k]))
        )
    sums, info = merge(parts)
    for k in range(ZS):
        at = slice(k * 8, k * 8 + 8)
        zo[k] = jnp.concatenate([sums[i][at] for i in range(4)], axis=0).astype(BF16)
        zw[k] = info[at]
    a_zs = []
    for k in range(1, ZS):
        a_zs.append(send(zo.at[z_at(k)], zo_in.at[k - 1], A_ZO + k - 1, z_peer(k)))
        a_zs.append(send(zw.at[z_at(k)], zw_in.at[k - 1], A_ZW + k - 1, z_peer(k)))

    g_c.wait_recv()
    for g in range(2):
        for j in range(7):
            at = slice(g * HALF + j * 128, g * HALF + j * 128 + 128)
            tile = jnp.where(c == g, h_t[:, j].reshape(32, 128), h_c[:, j].reshape(32, 128))
            hbf[:, at] = tile.astype(BF16)
    terms = dot_nt(hbf[...], wd[...])
    d_own[...] = jnp.concatenate([terms[0:16], terms[16:32]], axis=1)
    d_cps = [send(d_own, d_in.at[k - 1], G_TP + k, y_peer(k)) for k in range(1, TP)]
    forward(2, 0)
    forward(2, 1)

    def four(value):
        return [value[i * 8 : i * 8 + 8] for i in range(4)]

    arrive(a_zs)
    parts = [tree_part, (four(zo[z].astype(F32)), zw[z])]
    parts += [(four(zo_in[k].astype(F32)), zw_in[k]) for k in range(ZS - 1)]
    sums, info = merge(parts)
    for i in range(4):
        fin[i] = sums[i] / info[:, 4 + i : 5 + i]
    last = send(fin, fin_in, A_FIN, core_peer)
    arrive(d_cps)
    done = None
    for j in range(TP):
        slot = lax.rem(y - j + TP, TP)
        term = jnp.where(slot == 0, d_own[...], d_in[jnp.maximum(slot - 1, 0)])
        done = term if done is None else done + term
    draft_out[...] = jnp.concatenate([done[:, 0:64], done[:, 64:128]], axis=0).astype(BF16)
    last.wait_recv()
    for h in range(HEADS):
        tile = jnp.where(c == h // 4, fin[h % 4], fin_in[h % 4])
        attn_out[:, h * HD : (h + 1) * HD] = jnp.where(c == 0, tile[0:4], tile[4:8]).astype(BF16)

    arrive(m_z)
    for cp in kept:
        cp.wait()
    for cp in sent:
        cp.wait_send()


def place(attn, pages, draft, mc, attn_out, arrived, draft_out, after):
    me = lax.axis_index("ctx")

    def back(i, carry):
        s = 63 - i
        carry = jnp.where(mc[s, me] > 0, s, carry)
        after[s] = carry
        return carry

    after[64] = 64
    lax.fori_loop(0, 64, back, jnp.int32(64))

    def one(j, s):
        source = jnp.minimum(s, 63)
        kz = lax.rem(me // 2 - source // 2 + 64, ZS)
        kx = lax.rem(me // 16 - source // 16 + XS, XS)
        kc = lax.rem(me + source, 2)
        page = pages[kz, kx * 2 + kc]
        page = jnp.where(s < 64, page, jnp.zeros_like(page))
        arrived[pl.ds(pl.multiple_of(j * PAGE, PAGE), PAGE), :] = page
        return after[jnp.minimum(s + 1, 64)]

    lax.fori_loop(0, 32, one, after[0])
    attn_out[...] = attn[...]
    draft_out[...] = draft[...]


def body(
    kv_cache, page_session, queries, tree_kv, tree_parent, move_count,
    draft_states, accept_node, w_gate, w_up, w_down,
):
    vmem = pl.BlockSpec(memory_space=pltpu.VMEM)
    smem = pl.BlockSpec(memory_space=pltpu.SMEM)
    hbm = pl.BlockSpec(memory_space=pl.ANY)
    scratch = [
        pltpu.VMEM((SESS, 512, 128), BF16),
        pltpu.VMEM((SESS, 1, 4096), F32),
        pltpu.VMEM((512, 4096), F32),
        pltpu.VMEM((512, 128), F32),
        pltpu.VMEM((512, 128), F32),
        pltpu.VMEM((512, 128), F32),
        *[pltpu.VMEM((5, NODES, 128), F32)] * 4,
        pltpu.VMEM((4, 5, NODES, 128), F32),
        *[pltpu.VMEM((5, NODES, 128), F32)] * 4,
        *[pltpu.VMEM((256, 128), BF16)] * 3,
        *[pltpu.VMEM((8, 128), F32)] * 3,
        pltpu.VMEM((3, 256, 128), BF16),
        pltpu.VMEM((3, 8, 128), F32),
        pltpu.VMEM((ZS, 32, 128), BF16),
        pltpu.VMEM((ZS, 8, 128), F32),
        pltpu.VMEM((ZS - 1, 32, 128), BF16),
        pltpu.VMEM((ZS - 1, 8, 128), F32),
        pltpu.VMEM((4, 8, 128), F32),
        pltpu.VMEM((4, 8, 128), F32),
        pltpu.VMEM((2, XS, 8, 8, 256), F32),
        pltpu.VMEM((XS, 8, 8, 256), F32),
        pltpu.VMEM((XS, 64, 256), F32),
        pltpu.VMEM((XS - 1, 64, 256), F32),
        pltpu.VMEM((ZS, 8, 384), F32),
        pltpu.VMEM((ZS - 1, 8, 384), F32),
        pltpu.VMEM((8, 128), F32),
        pltpu.VMEM((ZS - 1, 8, 128), F32),
        pltpu.VMEM((7, 8, 128), F32),
        pltpu.VMEM((XS - 1, 7, 8, 128), F32),
        pltpu.VMEM((XS, 7, 8, 128), F32),
        pltpu.VMEM((XS, 7, 8, 128), F32),
        pltpu.VMEM((32, 1792), BF16),
        pltpu.VMEM((16, 128), F32),
        pltpu.VMEM((TP - 1, 16, 128), F32),
        pltpu.VMEM((XS, ZS, PAGE, 256), BF16),
        pltpu.VMEM((XS, ZS, PAGE, 256), BF16),
        pltpu.VMEM((XS, ZS, PAGE, 256), BF16),
        *[pltpu.VMEM((ZS, PAGE, 256), BF16)] * 6,
        pltpu.SemaphoreType.DMA((COPIES,)),
        pltpu.SemaphoreType.DMA((COPIES,)),
        pltpu.SemaphoreType.DMA((8,)),
    ]
    attn, pages, draft = pl.pallas_call(
        kernel,
        out_shape=(
            jax.ShapeDtypeStruct((4, 1024), BF16),
            jax.ShapeDtypeStruct((ZS, 8, PAGE, 256), BF16),
            jax.ShapeDtypeStruct((32, 64), BF16),
        ),
        in_specs=[vmem, smem, vmem, vmem, vmem, smem, vmem, smem, vmem, vmem, vmem],
        out_specs=(vmem, hbm, vmem),
        scratch_shapes=scratch,
        compiler_params=pltpu.CompilerParams(
            collective_id=0, has_side_effects=True, vmem_limit_bytes=56 * 1024 * 1024
        ),
        cost_estimate=pl.CostEstimate(
            flops=4 * 2048 * 4096 * 128, bytes_accessed=5 << 20, transcendentals=2048 * 4096
        ),
    )(
        kv_cache.reshape(64, PAGE, 256), page_session, queries, tree_kv, tree_parent, move_count,
        draft_states.T, accept_node, w_gate, w_up, w_down.T,
    )
    return pl.pallas_call(
        place,
        out_shape=(
            jax.ShapeDtypeStruct((4, 1024), BF16),
            jax.ShapeDtypeStruct((32 * PAGE, 256), BF16),
            jax.ShapeDtypeStruct((32, 64), BF16),
        ),
        in_specs=[vmem, vmem, vmem, smem],
        out_specs=(vmem, vmem, vmem),
        scratch_shapes=[pltpu.SMEM((65,), jnp.int32)],
        compiler_params=pltpu.CompilerParams(vmem_limit_bytes=16 * 1024 * 1024),
    )(attn, pages, draft, move_count)


def solution(mesh):
    placed = (
        P("ctx", "tp"),
        P("ctx"),
        P(None, "tp"),
        P(None, "tp"),
        P(),
        P(),
        P(None, "ctx"),
        P(),
        P("ctx", "tp"),
        P("ctx", "tp"),
        P("tp", "ctx"),
    )
    return jax.shard_map(
        body,
        mesh=mesh,
        in_specs=placed,
        out_specs=(P("ctx", "tp"), P("ctx", "tp"), P(None, "ctx")),
        check_vma=False,
    )
```

```python
import math

import jax
import jax.numpy as jnp
from jax import lax
from jax.experimental import pallas as pl
from jax.experimental.pallas import tpu as pltpu
from jax.sharding import PartitionSpec as P

MESH = pl.DeviceIdType.MESH
F32 = jnp.float32
BF16 = jnp.bfloat16

HD = 128
HEADS = 8
PAGE = 64
NODES = 64
SESS = 4
DD = 4096
XS, ZS, CS, TP = 4, 8, 2, 8
CHUNK = 512
FAR = -1e30
UNIT = math.log2(math.e) / math.sqrt(HD)
HALF = 896

F_CORE, F_X, F_Z = 0, 0, 3
G_CORE, G_Z, G_X, G_TP = 11, 11, 18, 21
A_CORE, A_XO, A_XW, A_ZO, A_ZW, A_FIN = 29, 32, 35, 38, 45, 53
M_CORE, M_X, M_Z = 54, 55, 61
COPIES = 61 + 8 * 7


def dot_nt(a, b):
    return lax.dot_general(a, b, (((1,), (1,)), ((), ())), preferred_element_type=F32)


def dot_nn(a, b):
    return jnp.dot(a, b, preferred_element_type=F32)


def merge(parts):
    n = parts[0][1].shape[0]
    spot = lax.broadcasted_iota(jnp.int32, (n, 128), 1)
    top = parts[0][1]
    for part in parts[1:]:
        top = jnp.maximum(top, part[1])
    total = None
    sums = [None] * 4
    for value, info in parts:
        factor = jnp.exp2(info - top)
        term = info * pltpu.roll(factor, 4, 1)
        total = term if total is None else total + term
        for i in range(4):
            term = value[i] * factor[:, i : i + 1]
            sums[i] = term if sums[i] is None else sums[i] + term
    return sums, jnp.where(spot < 4, top, jnp.where(spot < 8, total, 0.0))


def narrow(info):
    packed = info[0:8]
    for k in range(1, ZS):
        packed = packed + pltpu.roll(info[k * 8 : k * 8 + 8], 16 * k, 1)
    return packed


def widen(packed):
    spot = lax.broadcasted_iota(jnp.int32, (8, 128), 1)
    rows = [packed] + [pltpu.roll(packed, 128 - 16 * k, 1) for k in range(1, ZS)]
    return jnp.concatenate([jnp.where(spot < 8, row, 0.0) for row in rows], axis=0)


def split(info):
    high = info.astype(BF16).astype(F32)
    rest = info - high
    middle = rest.astype(BF16).astype(F32)
    both = high + pltpu.roll(middle, 8, 1)
    return jnp.concatenate([both, rest - middle], axis=0).astype(BF16)


def joined(tile):
    tile = tile.astype(F32)
    return tile[0:8] + pltpu.roll(tile[0:8], 120, 1) + tile[8:16]


def kernel(
    kv_h, ps, q_h, tkv_h, parent, mc, states, accept, wg_h, wu_h, wd_h, moves,
    attn_out, zin, draft_out, order,
    q2, bias, scores, mx, acc, tot,
    give0, give1, give2, give3, mine, core_in0, core_in1, core_in2, core_in3,
    xo0, xo1, xo2, xo_in, zo, zo_in, fin, fin_in,
    f_out, f_core, f_b, f_x, f_s, f_z, h_own, h_z, h_s, h_x, h_t, h_c, hbf, d_own, d_in,
    to_core, own_pages, from_core, xin0, xin1, xin2,
    kv, q, tkv, wg, wu, wd, blank, ssem, rsem, lsem, isem,
):
    give = [give0, give1, give2, give3]
    core_in = [core_in0, core_in1, core_in2, core_in3]
    xo = [xo0, xo1, xo2]
    xin = [xin0, xin1, xin2]
    me = lax.axis_index("ctx")
    y = lax.axis_index("tp")
    x = me // 16
    z = lax.rem(me // 2, 8)
    c = lax.rem(me, 2)

    def ctx_at(px, pz, pc):
        return {"ctx": px * 16 + pz * 2 + pc}

    core_peer = ctx_at(x, z, 1 - c)

    def x_at(k):
        return lax.rem(x + k, XS)

    def z_at(k):
        return lax.rem(z + k, ZS)

    def x_peer(k):
        return ctx_at(x_at(k), z, c)

    def z_peer(k):
        return ctx_at(x, z_at(k), c)

    def y_peer(k):
        return {"tp": lax.rem(y + k, TP)}

    sent = []

    def send(src, dst, i, peer):
        cp = pltpu.make_async_remote_copy(
            src_ref=src, dst_ref=dst, send_sem=ssem.at[i], recv_sem=rsem.at[i],
            device_id=peer, device_id_type=MESH,
        )
        cp.start()
        sent.append(cp)
        return cp

    def arrive(cps):
        for cp in cps:
            cp.wait_recv()

    barrier = pltpu.get_barrier_semaphore()
    peers = [core_peer] + [z_peer(k) for k in range(1, ZS)]
    peers += [x_peer(k) for k in range(1, XS)] + [y_peer(k) for k in range(1, TP)]
    for peer in peers:
        pl.semaphore_signal(barrier, inc=1, device_id=peer, device_id_type=MESH)

    loads = []
    for src, dst in ((wg_h, wg), (wu_h, wu), (kv_h, kv), (q_h, q), (tkv_h, tkv), (wd_h, wd)):
        cp = pltpu.make_async_copy(src, dst, isem.at[len(loads)])
        cp.start()
        loads.append(cp)

    sub = lax.broadcasted_iota(jnp.int32, (32, 256), 0)
    lane = lax.broadcasted_iota(jnp.int32, (32, 256), 1)
    row_of = jnp.zeros((32, 256), jnp.int32)
    for r in range(32):
        row_of = jnp.where(sub == r, accept[r // 8, r % 8] + (r // 8) * NODES, row_of)
    pick = jnp.where(lane == row_of, 1.0, 0.0).astype(BF16)
    chosen = dot_nt(pick, states[...])
    squares = jnp.broadcast_to(jnp.sum(chosen * chosen, axis=1, keepdims=True), (32, 256))
    chosen = chosen.astype(BF16)
    loads[0].wait()
    loads[1].wait()
    for half in range(2):
        gate = dot_nn(chosen, wg[:, half * HALF : (half + 1) * HALF])
        up = dot_nn(chosen, wu[:, half * HALF : (half + 1) * HALF])
        for px in range(XS):
            rows = slice(px * 8, px * 8 + 8)
            for j in range(7):
                cols = slice(j * 128, j * 128 + 128)
                f_out[half, px, j, :, 0:128] = gate[rows, cols]
                f_out[half, px, j, :, 128:256] = up[rows, cols]
            f_out[half, px, 7] = squares[rows, :]

    def pack(k, start):
        first = start
        second = start + mc[me, 2 * k]
        own = jnp.where(c == 0, first, second)
        other = jnp.where(c == 0, second, first)
        px, pz = k // ZS, lax.rem(k, ZS)
        own_pages[px, pz] = kv[own]
        to_core[px, pz] = kv[other]
        return second + mc[me, 2 * k + 1]

    loads[2].wait()
    lax.fori_loop(0, 32, pack, jnp.int32(0))

    pl.semaphore_wait(barrier, len(peers))

    z_order = (1, 7, 2, 6, 3, 5, 4)
    m_z = []
    kept = []
    blank[...] = jnp.zeros((PAGE, 256), BF16)
    cp = pltpu.make_async_copy(blank, zin.at[ZS, 0], lsem.at[8])
    cp.start()
    kept.append(cp)

    def send_group(src, group, lead=()):
        for k in z_order:
            m_z.append(
                send(src.at[(*lead, z_at(k))], zin.at[k, group], M_Z + group * 7 + k - 1, z_peer(k))
            )
        cp = pltpu.make_async_copy(src.at[(*lead, z)], zin.at[0, group], lsem.at[group])
        cp.start()
        kept.append(cp)

    f_cp = send(f_out.at[1 - c], f_core, F_CORE + 3, core_peer)
    m_core = send(to_core, from_core, M_CORE, core_peer)
    send_group(own_pages, 0, (x,))

    loads[3].wait()
    for s in range(SESS):
        for h in range(HEADS):
            q2[s, h * NODES : (h + 1) * NODES, :] = q[
                s * NODES : (s + 1) * NODES, h * HD : (h + 1) * HD
            ]
    lane1 = lax.broadcasted_iota(jnp.int32, (1, 128), 1)
    for t in range(32):
        session = jnp.where(lane1 < PAGE, ps[2 * t], ps[2 * t + 1])
        for s in range(SESS):
            bias[s, :, t * 128 : (t + 1) * 128] = jnp.where(session == s, 0.0, FAR).astype(F32)

    m_x = {}

    def send_x(k, part):
        src = own_pages if part == 0 else from_core
        m_x[k, part] = send(
            src.at[x_at(k)], xin[k - 1].at[part], M_X + (k - 1) * 2 + part, x_peer(k)
        )

    def forward(k, part):
        m_x[k, part].wait_recv()
        send_group(xin[k - 1], k * 2 + part, (part,))

    def attend(n, k):
        s = x_at(k)
        rows = q2[s]
        mx[...] = jnp.full((512, 128), FAR, F32)

        def first(t, carry):
            at = pl.ds(pl.multiple_of(t * CHUNK, CHUNK), CHUNK)
            pages = pl.ds(t * (CHUNK // PAGE), CHUNK // PAGE)
            keys = kv[pages, :, 0:HD].reshape(CHUNK, HD)
            part = dot_nt(rows, keys) + bias[s, :, at]
            scores[:, at] = part
            top = mx[...]
            for i in range(CHUNK // 128):
                top = jnp.maximum(top, part[:, i * 128 : (i + 1) * 128])
            mx[...] = top
            return carry

        lax.fori_loop(0, 4096 // CHUNK, first, 0)
        top = jnp.max(mx[...], axis=1, keepdims=True) * UNIT
        mx[...] = jnp.broadcast_to(top, (512, 128))
        acc[...] = jnp.zeros((512, 128), F32)
        tot[...] = jnp.zeros((512, 128), F32)

        def second(t, carry):
            at = pl.ds(pl.multiple_of(t * CHUNK, CHUNK), CHUNK)
            pages = pl.ds(t * (CHUNK // PAGE), CHUNK // PAGE)
            weight = jnp.exp2(scores[:, at] * UNIT - top)
            part = weight[:, 0:128]
            for i in range(1, CHUNK // 128):
                part = part + weight[:, i * 128 : (i + 1) * 128]
            tot[...] = tot[...] + part
            values = kv[pages, :, HD : 2 * HD].reshape(CHUNK, HD)
            acc[...] = acc[...] + dot_nn(weight.astype(BF16), values)
            return carry

        lax.fori_loop(0, 4096 // CHUNK, second, 0)
        tot[...] = jnp.broadcast_to(jnp.sum(tot[...], axis=1, keepdims=True), (512, 128))
        spot = lax.broadcasted_iota(jnp.int32, (NODES, 128), 1)
        for part, group in ((give[n], 1 - c), (mine.at[n], c)):
            info = jnp.zeros((NODES, 128), F32)
            for i in range(4):
                at = pl.ds(pl.multiple_of(group * 256 + i * NODES, NODES), NODES)
                part[i] = acc[at, :]
                info = jnp.where(spot == i, mx[at, :], info)
                info = jnp.where(spot == 4 + i, tot[at, :], info)
            part[4] = info
        return send(give[n], core_in[n], A_CORE + n if n < 3 else A_FIN - 1, core_peer)

    def part_of(ref):
        return [ref[i] for i in range(4)], ref[4]

    a_x = []

    def join(n, k, cp):
        cp.wait_recv()
        sums, info = merge([part_of(mine.at[n]), part_of(core_in[n])])
        if k == 0:
            for i in range(4):
                mine[n, i] = sums[i]
            mine[n, 4] = info
            return
        for i in range(4):
            xo[n][i * NODES : (i + 1) * NODES, :] = sums[i].astype(BF16)
        xo[n][256:272, :] = split(narrow(info))
        a_x.append(send(xo[n], xo_in.at[k - 1], A_XO + k - 1, x_peer(k)))

    f_cp.wait_recv()
    for px in range(XS):
        f_b[px] = (f_core[px] + f_out[c, px]).reshape(64, 256)
    f_xs = [send(f_b.at[x_at(k)], f_x.at[k - 1], F_X + k - 1, x_peer(k)) for k in range(1, XS)]
    send_x(1, 0)
    send_x(3, 0)
    m_core.wait_recv()
    send_group(from_core, 1, (x,))
    send_x(1, 1)
    send_x(3, 1)

    send_x(2, 0)
    send_x(2, 1)
    a0 = attend(0, 1)

    arrive(f_xs)
    whole = f_b[x]
    for k in range(XS - 1):
        whole = whole + f_x[k]
    for j in range(ZS):
        f_s[j, :, 0:256] = whole[j * 8 : j * 8 + 8]
        f_s[j, :, 256:384] = whole[56:64, 0:128]
    f_zs = [send(f_s.at[z_at(k)], f_z.at[k - 1], F_Z + k, z_peer(k)) for k in range(1, ZS)]
    join(0, 1, a0)
    forward(1, 0)
    forward(3, 0)

    a1 = attend(1, 3)

    arrive(f_zs)
    whole = f_s[z]
    for k in range(ZS - 1):
        whole = whole + f_z[k]
    inverse = lax.rsqrt(whole[:, 256:384] / DD + 1e-05)
    gate = inverse * whole[:, 0:128]
    up = inverse * whole[:, 128:256]
    hidden = gate / (1.0 + jnp.exp(-gate)) * up
    h_own[...] = hidden.astype(BF16).astype(F32)
    g_zs = [send(h_own, h_z.at[k - 1], G_Z + k, z_peer(k)) for k in range(1, ZS)]
    join(1, 3, a1)
    forward(1, 1)
    forward(3, 1)

    a2 = attend(2, 2)

    join(2, 2, a2)
    forward(2, 0)
    arrive(g_zs)
    for j in range(7):
        slot = lax.rem(z - j + ZS, ZS)
        h_s[j] = jnp.where(slot == 0, h_own[...], h_z[jnp.maximum(slot - 1, 0)])
    g_xs = [send(h_s, h_x.at[k - 1], G_X + k, x_peer(k)) for k in range(1, XS)]

    a3 = attend(3, 0)

    join(3, 0, a3)
    forward(2, 1)

    shard = lax.broadcasted_iota(jnp.int32, (64, 64), 0)
    other = lax.broadcasted_iota(jnp.int32, (64, 64), 1)
    count = jnp.sum(jnp.where(other == me, moves[...], 0).astype(F32), axis=1, keepdims=True)
    count = jnp.broadcast_to(count, (64, 128))
    rank = dot_nn(jnp.where(other < shard, 1.0, 0.0).astype(BF16), count.astype(BF16))
    shard = lax.broadcasted_iota(jnp.int32, (64, 128), 0)
    place_of = lax.broadcasted_iota(jnp.int32, (64, 128), 1).astype(F32)
    slot = lax.rem(z - lax.rem(shard // 2, ZS) + ZS, ZS) * 8
    slot = slot + lax.rem(x - shard // 16 + XS, XS) * 2 + lax.rem(c + shard, 2)
    hit = (rank == place_of) & (count > 0.5)
    found = jnp.sum(jnp.where(hit, slot.astype(F32) - 64.0, 0.0), axis=0, keepdims=True) + 64.0
    order[...] = jnp.broadcast_to(found, (8, 128)).astype(jnp.int32)

    link_at = lax.broadcasted_iota(jnp.int32, (NODES, NODES), 0)
    node_at = lax.broadcasted_iota(jnp.int32, (NODES, NODES), 1)
    link = jnp.where((parent[pl.ds(x, 1), :] == link_at) | (link_at == node_at), 1.0, 0.0)
    for repeat in range(6):
        link = jnp.minimum(dot_nn(link.astype(BF16), link.astype(BF16)), 1.0)
    own_row = lax.broadcasted_iota(jnp.int32, (32, NODES), 0)
    own_node = lax.broadcasted_iota(jnp.int32, (32, NODES), 1)
    own = jnp.where(own_node == z * 8 + lax.rem(own_row, 8), 1.0, 0.0).astype(BF16)
    reach = dot_nt(own, link.astype(BF16)) > 0.5
    loads[4].wait()
    loads[5].wait()
    block = pl.ds(pl.multiple_of(x * NODES, NODES), NODES)
    picks = []
    for i in range(4):
        rows = q2[x, pl.ds(pl.multiple_of(c * 256 + i * NODES, NODES), NODES), :]
        picks.append(dot_nn(own[0:8], rows))
    q_own = jnp.concatenate(picks, axis=0).astype(BF16)
    branch = jnp.where(reach, dot_nt(q_own, tkv[block, 0:HD]) * UNIT, FAR)
    tree_top = jnp.max(branch, axis=1, keepdims=True)
    weight = jnp.exp2(branch - tree_top)
    tree_total = jnp.sum(weight, axis=1, keepdims=True)
    tree_sum = dot_nn(weight.astype(BF16), tkv[block, HD : 2 * HD])
    spot8 = lax.broadcasted_iota(jnp.int32, (8, 128), 1)
    info = jnp.zeros((8, 128), F32)
    for i in range(4):
        at = slice(i * 8, i * 8 + 8)
        info = jnp.where(spot8 == i, tree_top[at], info)
        info = jnp.where(spot8 == 4 + i, tree_total[at], info)
    tree_part = ([tree_sum[i * 8 : i * 8 + 8] for i in range(4)], info)

    arrive(g_xs)
    for px in range(XS):
        slot = lax.rem(x - px + XS, XS)
        h_t[px] = jnp.where(slot == 0, h_s[...], h_x[jnp.maximum(slot - 1, 0)])
    g_c = send(h_t, h_c, G_CORE, core_peer)

    arrive(a_x)
    parts = [part_of(mine.at[3])]
    for k in range(XS - 1):
        value = xo_in[k, 0:256].astype(F32)
        parts.append(
            ([value[i * NODES : (i + 1) * NODES] for i in range(4)], widen(joined(xo_in[k, 256:272])))
        )
    sums, info = merge(parts)
    for k in range(ZS):
        at = slice(k * 8, k * 8 + 8)
        zo[k, 0:32] = jnp.concatenate([sums[i][at] for i in range(4)], axis=0).astype(BF16)
        zo[k, 32:48] = split(info[at])
    a_zs = []
    for k in range(1, ZS):
        a_zs.append(send(zo.at[z_at(k)], zo_in.at[k - 1], A_ZO + k - 1, z_peer(k)))

    g_c.wait_recv()
    for g in range(2):
        for j in range(7):
            at = slice(g * HALF + j * 128, g * HALF + j * 128 + 128)
            tile = jnp.where(c == g, h_t[:, j].reshape(32, 128), h_c[:, j].reshape(32, 128))
            hbf[:, at] = tile.astype(BF16)
    terms = dot_nt(hbf[...], wd[...])
    d_own[...] = jnp.concatenate([terms[0:16], terms[16:32]], axis=1)
    d_cps = [send(d_own, d_in.at[k - 1], G_TP + k, y_peer(k)) for k in range(1, TP)]

    def four(tile):
        value = tile[0:32].astype(F32)
        info = jnp.where(spot8 < 8, joined(tile[32:48]), 0.0)
        return [value[i * 8 : i * 8 + 8] for i in range(4)], info

    arrive(a_zs)
    parts = [tree_part, four(zo[z])] + [four(zo_in[k]) for k in range(ZS - 1)]
    sums, info = merge(parts)
    for i in range(4):
        fin[i] = sums[i] / info[:, 4 + i : 5 + i]
    last = send(fin, fin_in, A_FIN, core_peer)
    arrive(d_cps)
    done = None
    for j in range(TP):
        slot = lax.rem(y - j + TP, TP)
        term = jnp.where(slot == 0, d_own[...], d_in[jnp.maximum(slot - 1, 0)])
        done = term if done is None else done + term
    draft_out[...] = jnp.concatenate([done[:, 0:64], done[:, 64:128]], axis=0).astype(BF16)
    last.wait_recv()
    for h in range(HEADS):
        tile = jnp.where(c == h // 4, fin[h % 4], fin_in[h % 4])
        attn_out[:, h * HD : (h + 1) * HD] = jnp.where(c == 0, tile[0:4], tile[4:8]).astype(BF16)

    arrive(m_z)
    for cp in kept:
        cp.wait()
    for cp in sent:
        cp.wait_send()


def place(attn, pages, draft, order, attn_out, arrived, draft_out, held, sem):
    for j in range(32):
        pltpu.make_async_copy(pages.at[order[0, j]], held.at[j], sem.at[j // 16]).start()
    attn_out[...] = attn[...]
    draft_out[...] = draft[...]
    outs = []
    for half in range(2):
        part = pl.ds(half * 16, 16)
        pltpu.make_async_copy(held.at[part], held.at[part], sem.at[half]).wait()
        out = pltpu.make_async_copy(held.at[part], arrived.at[part], sem.at[2 + half])
        out.start()
        outs.append(out)
    for out in outs:
        out.wait()


def body(
    kv_cache, page_session, queries, tree_kv, tree_parent, move_count,
    draft_states, accept_node, w_gate, w_up, w_down,
):
    vmem = pl.BlockSpec(memory_space=pltpu.VMEM)
    smem = pl.BlockSpec(memory_space=pltpu.SMEM)
    hbm = pl.BlockSpec(memory_space=pl.ANY)
    scratch = [
        pltpu.VMEM((SESS, 512, 128), BF16),
        pltpu.VMEM((SESS, 1, 4096), F32),
        pltpu.VMEM((512, 4096), F32),
        pltpu.VMEM((512, 128), F32),
        pltpu.VMEM((512, 128), F32),
        pltpu.VMEM((512, 128), F32),
        *[pltpu.VMEM((5, NODES, 128), F32)] * 4,
        pltpu.VMEM((4, 5, NODES, 128), F32),
        *[pltpu.VMEM((5, NODES, 128), F32)] * 4,
        *[pltpu.VMEM((272, 128), BF16)] * 3,
        pltpu.VMEM((3, 272, 128), BF16),
        pltpu.VMEM((ZS, 48, 128), BF16),
        pltpu.VMEM((ZS - 1, 48, 128), BF16),
        pltpu.VMEM((4, 8, 128), F32),
        pltpu.VMEM((4, 8, 128), F32),
        pltpu.VMEM((2, XS, 8, 8, 256), F32),
        pltpu.VMEM((XS, 8, 8, 256), F32),
        pltpu.VMEM((XS, 64, 256), F32),
        pltpu.VMEM((XS - 1, 64, 256), F32),
        pltpu.VMEM((ZS, 8, 384), F32),
        pltpu.VMEM((ZS - 1, 8, 384), F32),
        pltpu.VMEM((8, 128), F32),
        pltpu.VMEM((ZS - 1, 8, 128), F32),
        pltpu.VMEM((7, 8, 128), F32),
        pltpu.VMEM((XS - 1, 7, 8, 128), F32),
        pltpu.VMEM((XS, 7, 8, 128), F32),
        pltpu.VMEM((XS, 7, 8, 128), F32),
        pltpu.VMEM((32, 1792), BF16),
        pltpu.VMEM((16, 128), F32),
        pltpu.VMEM((TP - 1, 16, 128), F32),
        pltpu.VMEM((XS, ZS, PAGE, 256), BF16),
        pltpu.VMEM((XS, ZS, PAGE, 256), BF16),
        pltpu.VMEM((XS, ZS, PAGE, 256), BF16),
        *[pltpu.VMEM((2, ZS, PAGE, 256), BF16)] * 3,
        pltpu.VMEM((64, PAGE, 256), BF16),
        pltpu.VMEM((256, 1024), BF16),
        pltpu.VMEM((256, 256), BF16),
        *[pltpu.VMEM((64, 1792), BF16)] * 3,
        pltpu.VMEM((PAGE, 256), BF16),
        pltpu.SemaphoreType.DMA((COPIES,)),
        pltpu.SemaphoreType.DMA((COPIES,)),
        pltpu.SemaphoreType.DMA((9,)),
        pltpu.SemaphoreType.DMA((6,)),
    ]
    attn, pages, draft, order = pl.pallas_call(
        kernel,
        out_shape=(
            jax.ShapeDtypeStruct((4, 1024), BF16),
            jax.ShapeDtypeStruct((ZS + 1, 8, PAGE, 256), BF16),
            jax.ShapeDtypeStruct((32, 64), BF16),
            jax.ShapeDtypeStruct((8, 128), jnp.int32),
        ),
        in_specs=[hbm, smem, hbm, hbm, vmem, smem, vmem, smem, hbm, hbm, hbm, vmem],
        out_specs=(vmem, hbm, vmem, vmem),
        scratch_shapes=scratch,
        compiler_params=pltpu.CompilerParams(
            collective_id=0, has_side_effects=True, vmem_limit_bytes=56 * 1024 * 1024
        ),
        cost_estimate=pl.CostEstimate(
            flops=4 * 2048 * 4096 * 128, bytes_accessed=5 << 20, transcendentals=2048 * 4096
        ),
    )(
        kv_cache.reshape(64, PAGE, 256), page_session, queries, tree_kv, tree_parent, move_count,
        draft_states.T, accept_node, w_gate, w_up, w_down.T,
        move_count,
    )
    attn, arrived, draft = pl.pallas_call(
        place,
        out_shape=(
            jax.ShapeDtypeStruct((4, 1024), BF16),
            jax.ShapeDtypeStruct((32, PAGE, 256), BF16),
            jax.ShapeDtypeStruct((32, 64), BF16),
        ),
        in_specs=[vmem, hbm, vmem, smem],
        out_specs=(vmem, hbm, vmem),
        scratch_shapes=[
            pltpu.VMEM((32, PAGE, 256), BF16),
            pltpu.SemaphoreType.DMA((4,)),
        ],
        compiler_params=pltpu.CompilerParams(vmem_limit_bytes=56 * 1024 * 1024),
    )(attn, pages.reshape(ZS * 8 + 8, PAGE, 256), draft, order)
    return attn, arrived.reshape(32 * PAGE, 256), draft


def solution(mesh):
    placed = (
        P("ctx", "tp"),
        P("ctx"),
        P(None, "tp"),
        P(None, "tp"),
        P(),
        P(),
        P(None, "ctx"),
        P(),
        P("ctx", "tp"),
        P("ctx", "tp"),
        P("tp", "ctx"),
    )
    return jax.shard_map(
        body,
        mesh=mesh,
        in_specs=placed,
        out_specs=(P("ctx", "tp"), P("ctx", "tp"), P(None, "ctx")),
        check_vma=False,
    )
```

```python
import math

import jax
import jax.numpy as jnp
from jax import lax
from jax.experimental import pallas as pl
from jax.experimental.pallas import tpu as pltpu
from jax.sharding import PartitionSpec as P

MESH = pl.DeviceIdType.MESH
F32 = jnp.float32
BF16 = jnp.bfloat16

HD = 128
HEADS = 8
PAGE = 64
NODES = 64
SESS = 4
DD = 4096
XS, ZS, CS, TP = 4, 8, 2, 8
CHUNK = 512
FAR = -1e30
UNIT = math.log2(math.e) / math.sqrt(HD)
HALF = 896

F_CORE, F_X, F_Z = 0, 0, 3
G_CORE, G_Z, G_X, G_TP = 11, 11, 18, 21
A_CORE, A_XO, A_XW, A_ZO, A_ZW, A_FIN = 29, 32, 35, 38, 45, 53
M_CORE, M_X, M_Z = 54, 55, 61
COPIES = 61 + 8 * 7


def dot_nt(a, b):
    return lax.dot_general(a, b, (((1,), (1,)), ((), ())), preferred_element_type=F32)


def dot_nn(a, b):
    return jnp.dot(a, b, preferred_element_type=F32)


def merge(parts):
    n = parts[0][1].shape[0]
    spot = lax.broadcasted_iota(jnp.int32, (n, 128), 1)
    top = parts[0][1]
    for part in parts[1:]:
        top = jnp.maximum(top, part[1])
    total = None
    sums = [None] * 4
    for value, info in parts:
        factor = jnp.exp2(info - top)
        term = info * pltpu.roll(factor, 4, 1)
        total = term if total is None else total + term
        for i in range(4):
            term = value[i] * factor[:, i : i + 1]
            sums[i] = term if sums[i] is None else sums[i] + term
    return sums, jnp.where(spot < 4, top, jnp.where(spot < 8, total, 0.0))


def narrow(info):
    packed = info[0:8]
    for k in range(1, ZS):
        packed = packed + pltpu.roll(info[k * 8 : k * 8 + 8], 16 * k, 1)
    return packed


def widen(packed):
    spot = lax.broadcasted_iota(jnp.int32, (8, 128), 1)
    rows = [packed] + [pltpu.roll(packed, 128 - 16 * k, 1) for k in range(1, ZS)]
    return jnp.concatenate([jnp.where(spot < 8, row, 0.0) for row in rows], axis=0)


def split(info):
    high = info.astype(BF16).astype(F32)
    rest = info - high
    middle = rest.astype(BF16).astype(F32)
    both = high + pltpu.roll(middle, 8, 1)
    return jnp.concatenate([both, rest - middle], axis=0).astype(BF16)


def joined(tile):
    tile = tile.astype(F32)
    return tile[0:8] + pltpu.roll(tile[0:8], 120, 1) + tile[8:16]


def kernel(
    kv_h, ps, q_h, tkv_h, parent, mc, states, accept, wg_h, wu_h, wd_h, moves,
    attn_out, zin, draft_out, order,
    q2, bias, scores, mx, acc, tot,
    give0, give1, give2, give3, mine, core_in0, core_in1, core_in2, core_in3,
    xo0, xo1, xo2, xo_in, zo, zo_in, fin, fin_in,
    f_out, f_core, f_b, f_x, f_s, f_z, h_own, h_z, h_s, h_x, h_t, h_c, hbf, d_own, d_in,
    to_core, own_pages, from_core, xin0, xin1, xin2,
    kv, q, tkv, wg, wu, wd, blank, ssem, rsem, lsem, isem,
):
    give = [give0, give1, give2, give3]
    core_in = [core_in0, core_in1, core_in2, core_in3]
    xo = [xo0, xo1, xo2]
    xin = [xin0, xin1, xin2]
    me = lax.axis_index("ctx")
    y = lax.axis_index("tp")
    x = me // 16
    z = lax.rem(me // 2, 8)
    c = lax.rem(me, 2)

    def ctx_at(px, pz, pc):
        return {"ctx": px * 16 + pz * 2 + pc}

    core_peer = ctx_at(x, z, 1 - c)

    def x_at(k):
        return lax.rem(x + k, XS)

    def z_at(k):
        return lax.rem(z + k, ZS)

    def x_peer(k):
        return ctx_at(x_at(k), z, c)

    def z_peer(k):
        return ctx_at(x, z_at(k), c)

    def y_peer(k):
        return {"tp": lax.rem(y + k, TP)}

    sent = []

    def send(src, dst, i, peer):
        cp = pltpu.make_async_remote_copy(
            src_ref=src, dst_ref=dst, send_sem=ssem.at[i], recv_sem=rsem.at[i],
            device_id=peer, device_id_type=MESH,
        )
        cp.start()
        sent.append(cp)
        return cp

    def arrive(cps):
        for cp in cps:
            cp.wait_recv()

    barrier = pltpu.get_barrier_semaphore()
    peers = [core_peer] + [z_peer(k) for k in range(1, ZS)]
    peers += [x_peer(k) for k in range(1, XS)] + [y_peer(k) for k in range(1, TP)]
    for peer in peers:
        pl.semaphore_signal(barrier, inc=1, device_id=peer, device_id_type=MESH)

    loads = []
    for src, dst in ((wg_h, wg), (wu_h, wu), (kv_h, kv), (q_h, q), (tkv_h, tkv), (wd_h, wd)):
        cp = pltpu.make_async_copy(src, dst, isem.at[len(loads)])
        cp.start()
        loads.append(cp)

    sub = lax.broadcasted_iota(jnp.int32, (32, 256), 0)
    lane = lax.broadcasted_iota(jnp.int32, (32, 256), 1)
    row_of = jnp.zeros((32, 256), jnp.int32)
    for r in range(32):
        row_of = jnp.where(sub == r, accept[r // 8, r % 8] + (r // 8) * NODES, row_of)
    pick = jnp.where(lane == row_of, 1.0, 0.0).astype(BF16)
    chosen = dot_nt(pick, states[...])
    squares = jnp.broadcast_to(jnp.sum(chosen * chosen, axis=1, keepdims=True), (32, 256))
    chosen = chosen.astype(BF16)
    loads[0].wait()
    loads[1].wait()
    for half in range(2):
        gate = dot_nn(chosen, wg[:, half * HALF : (half + 1) * HALF])
        up = dot_nn(chosen, wu[:, half * HALF : (half + 1) * HALF])
        for px in range(XS):
            rows = slice(px * 8, px * 8 + 8)
            for j in range(7):
                cols = slice(j * 128, j * 128 + 128)
                f_out[half, px, j, :, 0:128] = gate[rows, cols]
                f_out[half, px, j, :, 128:256] = up[rows, cols]
            f_out[half, px, 7] = squares[rows, :]

    def pack(k, start):
        first = start
        second = start + mc[me, 2 * k]
        own = jnp.where(c == 0, first, second)
        other = jnp.where(c == 0, second, first)
        px, pz = k // ZS, lax.rem(k, ZS)
        own_pages[px, pz] = kv[own]
        to_core[px, pz] = kv[other]
        return second + mc[me, 2 * k + 1]

    loads[2].wait()
    lax.fori_loop(0, 32, pack, jnp.int32(0))

    pl.semaphore_wait(barrier, len(peers))

    z_order = (1, 7, 2, 6, 3, 5, 4)
    m_z = []
    kept = []
    blank[...] = jnp.zeros((PAGE, 256), BF16)
    cp = pltpu.make_async_copy(blank, zin.at[ZS, 0], lsem.at[8])
    cp.start()
    kept.append(cp)

    def send_group(src, group, lead=()):
        for k in z_order:
            m_z.append(
                send(src.at[(*lead, z_at(k))], zin.at[k, group], M_Z + group * 7 + k - 1, z_peer(k))
            )
        cp = pltpu.make_async_copy(src.at[(*lead, z)], zin.at[0, group], lsem.at[group])
        cp.start()
        kept.append(cp)

    f_cp = send(f_out.at[1 - c], f_core, F_CORE + 3, core_peer)
    m_core = send(to_core, from_core, M_CORE, core_peer)
    send_group(own_pages, 0, (x,))

    loads[3].wait()
    for s in range(SESS):
        for h in range(HEADS):
            q2[s, h * NODES : (h + 1) * NODES, :] = q[
                s * NODES : (s + 1) * NODES, h * HD : (h + 1) * HD
            ]
    lane1 = lax.broadcasted_iota(jnp.int32, (1, 128), 1)
    for t in range(32):
        session = jnp.where(lane1 < PAGE, ps[2 * t], ps[2 * t + 1])
        for s in range(SESS):
            bias[s, :, t * 128 : (t + 1) * 128] = jnp.where(session == s, 0.0, FAR).astype(F32)

    m_x = {}

    def send_x(k, part):
        src = own_pages if part == 0 else from_core
        m_x[k, part] = send(
            src.at[x_at(k)], xin[k - 1].at[part], M_X + (k - 1) * 2 + part, x_peer(k)
        )

    def forward(k, part):
        m_x[k, part].wait_recv()
        send_group(xin[k - 1], k * 2 + part, (part,))

    def attend(n, k):
        s = x_at(k)
        rows = q2[s]
        mx[...] = jnp.full((512, 128), FAR, F32)

        def first(t, carry):
            at = pl.ds(pl.multiple_of(t * CHUNK, CHUNK), CHUNK)
            pages = pl.ds(t * (CHUNK // PAGE), CHUNK // PAGE)
            keys = kv[pages, :, 0:HD].reshape(CHUNK, HD)
            part = dot_nt(rows, keys) + bias[s, :, at]
            scores[:, at] = part
            top = mx[...]
            for i in range(CHUNK // 128):
                top = jnp.maximum(top, part[:, i * 128 : (i + 1) * 128])
            mx[...] = top
            return carry

        lax.fori_loop(0, 4096 // CHUNK, first, 0)
        top = jnp.max(mx[...], axis=1, keepdims=True) * UNIT
        mx[...] = jnp.broadcast_to(top, (512, 128))
        acc[...] = jnp.zeros((512, 128), F32)
        tot[...] = jnp.zeros((512, 128), F32)

        def second(t, carry):
            at = pl.ds(pl.multiple_of(t * CHUNK, CHUNK), CHUNK)
            pages = pl.ds(t * (CHUNK // PAGE), CHUNK // PAGE)
            weight = jnp.exp2(scores[:, at] * UNIT - top)
            part = weight[:, 0:128]
            for i in range(1, CHUNK // 128):
                part = part + weight[:, i * 128 : (i + 1) * 128]
            tot[...] = tot[...] + part
            values = kv[pages, :, HD : 2 * HD].reshape(CHUNK, HD)
            acc[...] = acc[...] + dot_nn(weight.astype(BF16), values)
            return carry

        lax.fori_loop(0, 4096 // CHUNK, second, 0)
        tot[...] = jnp.broadcast_to(jnp.sum(tot[...], axis=1, keepdims=True), (512, 128))
        spot = lax.broadcasted_iota(jnp.int32, (NODES, 128), 1)
        for part, group in ((give[n], 1 - c), (mine.at[n], c)):
            info = jnp.zeros((NODES, 128), F32)
            for i in range(4):
                at = pl.ds(pl.multiple_of(group * 256 + i * NODES, NODES), NODES)
                part[i] = acc[at, :]
                info = jnp.where(spot == i, mx[at, :], info)
                info = jnp.where(spot == 4 + i, tot[at, :], info)
            part[4] = info
        return send(give[n], core_in[n], A_CORE + n if n < 3 else A_FIN - 1, core_peer)

    def part_of(ref):
        return [ref[i] for i in range(4)], ref[4]

    a_x = []

    def join(n, k, cp):
        cp.wait_recv()
        sums, info = merge([part_of(mine.at[n]), part_of(core_in[n])])
        if k == 0:
            for i in range(4):
                mine[n, i] = sums[i]
            mine[n, 4] = info
            return
        for i in range(4):
            xo[n][i * NODES : (i + 1) * NODES, :] = sums[i].astype(BF16)
        xo[n][256:272, :] = split(narrow(info))
        a_x.append(send(xo[n], xo_in.at[k - 1], A_XO + k - 1, x_peer(k)))

    f_cp.wait_recv()
    for px in range(XS):
        f_b[px] = (f_core[px] + f_out[c, px]).reshape(64, 256)
    f_xs = [send(f_b.at[x_at(k)], f_x.at[k - 1], F_X + k - 1, x_peer(k)) for k in range(1, XS)]
    send_x(1, 0)
    send_x(3, 0)
    m_core.wait_recv()
    send_group(from_core, 1, (x,))
    send_x(1, 1)
    send_x(3, 1)

    send_x(2, 0)
    send_x(2, 1)
    a0 = attend(0, 1)

    arrive(f_xs)
    whole = f_b[x]
    for k in range(XS - 1):
        whole = whole + f_x[k]
    for j in range(ZS):
        f_s[j, :, 0:256] = whole[j * 8 : j * 8 + 8]
        f_s[j, :, 256:384] = whole[56:64, 0:128]
    f_zs = [send(f_s.at[z_at(k)], f_z.at[k - 1], F_Z + k, z_peer(k)) for k in range(1, ZS)]
    join(0, 1, a0)
    forward(1, 0)
    forward(3, 0)

    a1 = attend(1, 3)

    arrive(f_zs)
    whole = f_s[z]
    for k in range(ZS - 1):
        whole = whole + f_z[k]
    inverse = lax.rsqrt(whole[:, 256:384] / DD + 1e-05)
    gate = inverse * whole[:, 0:128]
    up = inverse * whole[:, 128:256]
    hidden = gate / (1.0 + jnp.exp(-gate)) * up
    h_own[...] = hidden.astype(BF16).astype(F32)
    g_zs = [send(h_own, h_z.at[k - 1], G_Z + k, z_peer(k)) for k in range(1, ZS)]
    join(1, 3, a1)
    forward(1, 1)
    forward(3, 1)

    a2 = attend(2, 2)

    join(2, 2, a2)
    arrive(g_zs)
    for j in range(7):
        slot = lax.rem(z - j + ZS, ZS)
        h_s[j] = jnp.where(slot == 0, h_own[...], h_z[jnp.maximum(slot - 1, 0)])
    g_xs = [send(h_s, h_x.at[k - 1], G_X + k, x_peer(k)) for k in range(1, XS)]

    a3 = attend(3, 0)

    join(3, 0, a3)
    forward(2, 0)

    shard = lax.broadcasted_iota(jnp.int32, (64, 64), 0)
    other = lax.broadcasted_iota(jnp.int32, (64, 64), 1)
    count = jnp.sum(jnp.where(other == me, moves[...], 0).astype(F32), axis=1, keepdims=True)
    count = jnp.broadcast_to(count, (64, 128))
    rank = dot_nn(jnp.where(other < shard, 1.0, 0.0).astype(BF16), count.astype(BF16))
    shard = lax.broadcasted_iota(jnp.int32, (64, 128), 0)
    place_of = lax.broadcasted_iota(jnp.int32, (64, 128), 1).astype(F32)
    slot = lax.rem(z - lax.rem(shard // 2, ZS) + ZS, ZS) * 8
    slot = slot + lax.rem(x - shard // 16 + XS, XS) * 2 + lax.rem(c + shard, 2)
    hit = (rank == place_of) & (count > 0.5)
    found = jnp.sum(jnp.where(hit, slot.astype(F32) - 64.0, 0.0), axis=0, keepdims=True) + 64.0
    order[...] = jnp.broadcast_to(found, (8, 128)).astype(jnp.int32)

    link_at = lax.broadcasted_iota(jnp.int32, (NODES, NODES), 0)
    node_at = lax.broadcasted_iota(jnp.int32, (NODES, NODES), 1)
    link = jnp.where((parent[pl.ds(x, 1), :] == link_at) | (link_at == node_at), 1.0, 0.0)
    for repeat in range(6):
        link = jnp.minimum(dot_nn(link.astype(BF16), link.astype(BF16)), 1.0)
    own_row = lax.broadcasted_iota(jnp.int32, (32, NODES), 0)
    own_node = lax.broadcasted_iota(jnp.int32, (32, NODES), 1)
    own = jnp.where(own_node == z * 8 + lax.rem(own_row, 8), 1.0, 0.0).astype(BF16)
    reach = dot_nt(own, link.astype(BF16)) > 0.5
    loads[4].wait()
    loads[5].wait()
    block = pl.ds(pl.multiple_of(x * NODES, NODES), NODES)
    picks = []
    for i in range(4):
        rows = q2[x, pl.ds(pl.multiple_of(c * 256 + i * NODES, NODES), NODES), :]
        picks.append(dot_nn(own[0:8], rows))
    q_own = jnp.concatenate(picks, axis=0).astype(BF16)
    branch = jnp.where(reach, dot_nt(q_own, tkv[block, 0:HD]) * UNIT, FAR)
    tree_top = jnp.max(branch, axis=1, keepdims=True)
    weight = jnp.exp2(branch - tree_top)
    tree_total = jnp.sum(weight, axis=1, keepdims=True)
    tree_sum = dot_nn(weight.astype(BF16), tkv[block, HD : 2 * HD])
    spot8 = lax.broadcasted_iota(jnp.int32, (8, 128), 1)
    info = jnp.zeros((8, 128), F32)
    for i in range(4):
        at = slice(i * 8, i * 8 + 8)
        info = jnp.where(spot8 == i, tree_top[at], info)
        info = jnp.where(spot8 == 4 + i, tree_total[at], info)
    tree_part = ([tree_sum[i * 8 : i * 8 + 8] for i in range(4)], info)

    forward(2, 1)
    arrive(g_xs)
    for px in range(XS):
        slot = lax.rem(x - px + XS, XS)
        h_t[px] = jnp.where(slot == 0, h_s[...], h_x[jnp.maximum(slot - 1, 0)])
    g_c = send(h_t, h_c, G_CORE, core_peer)

    arrive(a_x)
    parts = [part_of(mine.at[3])]
    for k in range(XS - 1):
        value = xo_in[k, 0:256].astype(F32)
        parts.append(
            ([value[i * NODES : (i + 1) * NODES] for i in range(4)], widen(joined(xo_in[k, 256:272])))
        )
    sums, info = merge(parts)
    for k in range(ZS):
        at = slice(k * 8, k * 8 + 8)
        zo[k, 0:32] = jnp.concatenate([sums[i][at] for i in range(4)], axis=0).astype(BF16)
        zo[k, 32:48] = split(info[at])
    a_zs = []
    for k in range(1, ZS):
        a_zs.append(send(zo.at[z_at(k)], zo_in.at[k - 1], A_ZO + k - 1, z_peer(k)))

    g_c.wait_recv()
    for g in range(2):
        for j in range(7):
            at = slice(g * HALF + j * 128, g * HALF + j * 128 + 128)
            tile = jnp.where(c == g, h_t[:, j].reshape(32, 128), h_c[:, j].reshape(32, 128))
            hbf[:, at] = tile.astype(BF16)
    terms = dot_nt(hbf[...], wd[...])
    d_own[...] = jnp.concatenate([terms[0:16], terms[16:32]], axis=1)
    d_cps = [send(d_own, d_in.at[k - 1], G_TP + k, y_peer(k)) for k in range(1, TP)]

    def four(tile):
        value = tile[0:32].astype(F32)
        info = jnp.where(spot8 < 8, joined(tile[32:48]), 0.0)
        return [value[i * 8 : i * 8 + 8] for i in range(4)], info

    arrive(a_zs)
    parts = [tree_part, four(zo[z])] + [four(zo_in[k]) for k in range(ZS - 1)]
    sums, info = merge(parts)
    for i in range(4):
        fin[i] = sums[i] / info[:, 4 + i : 5 + i]
    last = send(fin, fin_in, A_FIN, core_peer)
    arrive(d_cps)
    done = None
    for j in range(TP):
        slot = lax.rem(y - j + TP, TP)
        term = jnp.where(slot == 0, d_own[...], d_in[jnp.maximum(slot - 1, 0)])
        done = term if done is None else done + term
    draft_out[...] = jnp.concatenate([done[:, 0:64], done[:, 64:128]], axis=0).astype(BF16)
    last.wait_recv()
    for h in range(HEADS):
        tile = jnp.where(c == h // 4, fin[h % 4], fin_in[h % 4])
        attn_out[:, h * HD : (h + 1) * HD] = jnp.where(c == 0, tile[0:4], tile[4:8]).astype(BF16)

    arrive(m_z)
    for cp in kept:
        cp.wait()
    for cp in sent:
        cp.wait_send()


def place(attn, pages, draft, order, attn_out, arrived, draft_out, held, sem):
    for j in range(32):
        pltpu.make_async_copy(pages.at[order[0, j]], held.at[j], sem.at[j // 16]).start()
    attn_out[...] = attn[...]
    draft_out[...] = draft[...]
    outs = []
    for half in range(2):
        part = pl.ds(half * 16, 16)
        pltpu.make_async_copy(held.at[part], held.at[part], sem.at[half]).wait()
        out = pltpu.make_async_copy(held.at[part], arrived.at[part], sem.at[2 + half])
        out.start()
        outs.append(out)
    for out in outs:
        out.wait()


def body(
    kv_cache, page_session, queries, tree_kv, tree_parent, move_count,
    draft_states, accept_node, w_gate, w_up, w_down,
):
    vmem = pl.BlockSpec(memory_space=pltpu.VMEM)
    smem = pl.BlockSpec(memory_space=pltpu.SMEM)
    hbm = pl.BlockSpec(memory_space=pl.ANY)
    scratch = [
        pltpu.VMEM((SESS, 512, 128), BF16),
        pltpu.VMEM((SESS, 1, 4096), F32),
        pltpu.VMEM((512, 4096), F32),
        pltpu.VMEM((512, 128), F32),
        pltpu.VMEM((512, 128), F32),
        pltpu.VMEM((512, 128), F32),
        *[pltpu.VMEM((5, NODES, 128), F32)] * 4,
        pltpu.VMEM((4, 5, NODES, 128), F32),
        *[pltpu.VMEM((5, NODES, 128), F32)] * 4,
        *[pltpu.VMEM((272, 128), BF16)] * 3,
        pltpu.VMEM((3, 272, 128), BF16),
        pltpu.VMEM((ZS, 48, 128), BF16),
        pltpu.VMEM((ZS - 1, 48, 128), BF16),
        pltpu.VMEM((4, 8, 128), F32),
        pltpu.VMEM((4, 8, 128), F32),
        pltpu.VMEM((2, XS, 8, 8, 256), F32),
        pltpu.VMEM((XS, 8, 8, 256), F32),
        pltpu.VMEM((XS, 64, 256), F32),
        pltpu.VMEM((XS - 1, 64, 256), F32),
        pltpu.VMEM((ZS, 8, 384), F32),
        pltpu.VMEM((ZS - 1, 8, 384), F32),
        pltpu.VMEM((8, 128), F32),
        pltpu.VMEM((ZS - 1, 8, 128), F32),
        pltpu.VMEM((7, 8, 128), F32),
        pltpu.VMEM((XS - 1, 7, 8, 128), F32),
        pltpu.VMEM((XS, 7, 8, 128), F32),
        pltpu.VMEM((XS, 7, 8, 128), F32),
        pltpu.VMEM((32, 1792), BF16),
        pltpu.VMEM((16, 128), F32),
        pltpu.VMEM((TP - 1, 16, 128), F32),
        pltpu.VMEM((XS, ZS, PAGE, 256), BF16),
        pltpu.VMEM((XS, ZS, PAGE, 256), BF16),
        pltpu.VMEM((XS, ZS, PAGE, 256), BF16),
        *[pltpu.VMEM((2, ZS, PAGE, 256), BF16)] * 3,
        pltpu.VMEM((64, PAGE, 256), BF16),
        pltpu.VMEM((256, 1024), BF16),
        pltpu.VMEM((256, 256), BF16),
        *[pltpu.VMEM((64, 1792), BF16)] * 3,
        pltpu.VMEM((PAGE, 256), BF16),
        pltpu.SemaphoreType.DMA((COPIES,)),
        pltpu.SemaphoreType.DMA((COPIES,)),
        pltpu.SemaphoreType.DMA((9,)),
        pltpu.SemaphoreType.DMA((6,)),
    ]
    attn, pages, draft, order = pl.pallas_call(
        kernel,
        out_shape=(
            jax.ShapeDtypeStruct((4, 1024), BF16),
            jax.ShapeDtypeStruct((ZS + 1, 8, PAGE, 256), BF16),
            jax.ShapeDtypeStruct((32, 64), BF16),
            jax.ShapeDtypeStruct((8, 128), jnp.int32),
        ),
        in_specs=[hbm, smem, hbm, hbm, vmem, smem, vmem, smem, hbm, hbm, hbm, vmem],
        out_specs=(vmem, hbm, vmem, vmem),
        scratch_shapes=scratch,
        compiler_params=pltpu.CompilerParams(
            collective_id=0, has_side_effects=True, vmem_limit_bytes=56 * 1024 * 1024
        ),
        cost_estimate=pl.CostEstimate(
            flops=4 * 2048 * 4096 * 128, bytes_accessed=5 << 20, transcendentals=2048 * 4096
        ),
    )(
        kv_cache.reshape(64, PAGE, 256), page_session, queries, tree_kv, tree_parent, move_count,
        draft_states.T, accept_node, w_gate, w_up, w_down.T,
        move_count,
    )
    attn, arrived, draft = pl.pallas_call(
        place,
        out_shape=(
            jax.ShapeDtypeStruct((4, 1024), BF16),
            jax.ShapeDtypeStruct((32, PAGE, 256), BF16),
            jax.ShapeDtypeStruct((32, 64), BF16),
        ),
        in_specs=[vmem, hbm, vmem, smem],
        out_specs=(vmem, hbm, vmem),
        scratch_shapes=[
            pltpu.VMEM((32, PAGE, 256), BF16),
            pltpu.SemaphoreType.DMA((4,)),
        ],
        compiler_params=pltpu.CompilerParams(vmem_limit_bytes=56 * 1024 * 1024),
    )(attn, pages.reshape(ZS * 8 + 8, PAGE, 256), draft, order)
    return attn, arrived.reshape(32 * PAGE, 256), draft


def solution(mesh):
    placed = (
        P("ctx", "tp"),
        P("ctx"),
        P(None, "tp"),
        P(None, "tp"),
        P(),
        P(),
        P(None, "ctx"),
        P(),
        P("ctx", "tp"),
        P("ctx", "tp"),
        P("tp", "ctx"),
    )
    return jax.shard_map(
        body,
        mesh=mesh,
        in_specs=placed,
        out_specs=(P("ctx", "tp"), P("ctx", "tp"), P(None, "ctx")),
        check_vma=False,
    )
```
